512 devices in a mesh: lag: 16 (over x, y_lo, core), row: 32 (over y_hi, z).
Axes of the slice: x: 4, y: 8 (y_hi: 4, y_lo: 2; y = y_hi * 2 + y_lo), z: 8, core: 2. Of those that a mesh axis runs over, the one named last changes fastest.
Arguments:
- currents: bfloat16 [2048, 4096], P('lag', 'row'), may hold values from -6 to 6
- panels: bfloat16 [16, 4096, 4096], P('lag', 'row'), may hold values from -0.09375 to 0.09375
- excitation: float32 [2048, 4096], P('lag', 'row'), may hold values from -6 to 6
Outputs:
- residual: float32 [2048, 4096], P('lag', 'row')
The draws below stay inside these ranges and needn't reach their ends.
All inputs are finite; a program needn't handle non-finite values.
Results may differ from the reference program's by a relative error of at most 0.0003.
Values may be sent and summed in bfloat16 or wider, within the bound.
No kernel may reach another device: no remote copies, remote signals or barrier semaphores. Data moves between devices by JAX's collectives and lax.ppermute only.
A program may use at most 64 MiB of HBM per device.

```python
import jax
import jax.numpy as jnp
from jax import lax

N = 4096
LAGS = 16
TIMES = 2048


def level_of(key, shape, shards, low, largest):
    def one(position, blocks):
        steps = jax.random.uniform(jax.random.fold_in(jax.random.fold_in(key, 6), position), (blocks,), jnp.float32, low / len(shards), largest / len(shards))
        return jnp.repeat(jnp.exp(steps), shape[position] // blocks).reshape((-1,) + (1,) * (len(shape) - position - 1))

    loudness = one(*shards[0])
    for cut in shards[1:]:
        loudness = loudness * one(*cut)
    return loudness


def centred(stream_key, shape, deviation, bound, cuts=(), kind=jnp.bfloat16):
    factor_of = level_of(stream_key, shape, cuts, -0.22, 0.18) if cuts else 1.0
    drawn = jax.random.normal(stream_key, shape, jnp.float32) * deviation * factor_of
    return jnp.minimum(jnp.maximum(drawn, -bound), bound).astype(kind)


def setup_inputs(seed: int = 0) -> dict:
    keys = jax.random.split(jax.random.key(seed), 4)
    currents = centred(keys[0], (TIMES, N), 1.0, 6.0, ((0, 16), (1, 32)))
    panels = centred(keys[1], (LAGS, N, N), N ** -0.5, 0.09375, ((0, 16), (1, 32)))
    excitation = centred(keys[2], (TIMES, N), 1.0, 6.0, ((0, 16), (1, 32)), jnp.float32)
    return {"currents": currents, "panels": panels, "excitation": excitation}


def reference(currents, panels, excitation):
    padded = jnp.concatenate([jnp.zeros((LAGS - 1, N), jnp.bfloat16), currents], 0)

    def add_term(running, k):
        shifted = lax.dynamic_slice_in_dim(padded, (LAGS - 1 - k).astype(jnp.int32), TIMES, 0)
        matrix = lax.dynamic_index_in_dim(panels, k.astype(jnp.int32), 0, keepdims=False)
        product = lax.dot_general(shifted, matrix, (((1,), (1,)), ((), ())), preferred_element_type=jnp.float32)
        return running + product, None

    field, _ = lax.scan(add_term, jnp.zeros((TIMES, N), jnp.float32), jnp.arange(LAGS, dtype=jnp.int32))
    return excitation - field
```

```python
import jax
import jax.numpy as jnp
from jax import lax
from jax.experimental import pallas as pl
from jax.experimental.pallas import tpu as pltpu
from jax.sharding import Mesh, PartitionSpec as P

B = 128
HALO = 16
LAGS = 16
LAG = ("x", "yl", "c")
ROW = ("yh", "zh", "zl")
TRADE = ("x", "yl", "zl")
COPIES = ("yh", "zh")


def swap_pairs():
    pairs = []
    for x in range(4):
        for yl in range(2):
            for c in range(2):
                for yh in range(4):
                    for zh in range(4):
                        for zl in range(2):
                            src = ((x * 2 + yl) * 2 + c) * 32 + yh * 8 + zh * 2 + zl
                            to_z = (zh // 2) * 2 + yl
                            dst = ((yh * 2 + zh % 2) * 2 + c) * 32 + x * 8 + to_z * 2 + zl
                            pairs.append((src, dst))
    return pairs


def split_kernel(p_ref, o_ref):
    for x in range(4):
        for yl in range(2):
            for zl in range(2):
                for h in range(2):
                    col = (x * 8 + h * 4 + yl * 2 + zl) * B
                    o_ref[(x * 2 + yl) * 2 + zl, :, h * B:(h + 1) * B] = p_ref[0, :, col:col + B]


def split_panels(panels):
    vmem = pl.BlockSpec(memory_space=pltpu.VMEM)
    return pl.pallas_call(
        split_kernel,
        out_shape=jax.ShapeDtypeStruct((16, B, 2 * B), jnp.bfloat16),
        in_specs=[vmem],
        out_specs=vmem,
        name="split",
    )(panels)


def field_kernel(c_ref, own_ref, other_ref, x_ref, out_ref, w_ref, a_ref):
    core = c_ref[0]
    for k in range(8):
        w_ref[2 * k + core] = own_ref[k]
        w_ref[2 * k + 1 - core] = other_ref[k]
    for m in range(8):
        for h in range(2):
            slab = x_ref[(m // 2) * 4 + h * 2 + m % 2].astype(jnp.float32)
            for k in range(LAGS):
                a_ref[m * B:(m + 1) * B, (2 * k + h) * B:(2 * k + h + 1) * B] = slab[HALO - k:HALO - k + B].astype(jnp.bfloat16)
    for s in range(2):
        acc = jnp.zeros((4 * B, 2 * B), jnp.float32)
        for k in range(LAGS):
            acc += lax.dot_general(
                a_ref[s * 4 * B:(s + 1) * 4 * B, k * 2 * B:(k + 1) * 2 * B], w_ref[k], (((1,), (1,)), ((), ())), preferred_element_type=jnp.float32
            )
        for m in range(4):
            for zl in range(2):
                out_ref[(s * 4 + m) * 2 + zl] = acc[m * B:(m + 1) * B, zl * B:(zl + 1) * B].astype(out_ref.dtype)


def field_of(core, own, other, x):
    vmem = pl.BlockSpec(memory_space=pltpu.VMEM)
    return pl.pallas_call(
        field_kernel,
        out_shape=jax.ShapeDtypeStruct((16, B, B), jnp.float32),
        in_specs=[pl.BlockSpec(memory_space=pltpu.SMEM), vmem, vmem, vmem],
        out_specs=vmem,
        scratch_shapes=[
            pltpu.VMEM((LAGS, 2 * B, 2 * B), jnp.bfloat16),
            pltpu.VMEM((8 * B, LAGS * 2 * B), jnp.bfloat16),
        ],
        compiler_params=pltpu.CompilerParams(vmem_limit_bytes=48 * 1024 * 1024),
        name="field",
    )(core, own, other, x)


def body(currents, panels, excitation):
    halo = lax.ppermute(currents[B - HALO:], LAG, [(i, i + 1) for i in range(15)])
    piece = jnp.concatenate([halo, currents], 0)
    own = lax.all_to_all(split_panels(panels), TRADE, 0, 0, tiled=True).reshape(8, 2 * B, 2 * B)
    piece = lax.ppermute(piece, LAG + ROW, swap_pairs())
    x = lax.all_to_all(jnp.broadcast_to(piece[None], (16,) + piece.shape), COPIES, 0, 0, tiled=True)
    other = lax.ppermute(own, "c", [(0, 1), (1, 0)])
    core = lax.axis_index("c").astype(jnp.int32).reshape(1)
    part = field_of(core, own, other, x).astype(jnp.float16)
    got = lax.all_to_all(part, TRADE, 0, 0, tiled=True)
    return excitation - jnp.sum(got.astype(jnp.float32), 0)


def solution(mesh):
    fine = Mesh(mesh.devices.reshape(4, 2, 2, 4, 4, 2), LAG + ROW)
    return jax.shard_map(
        body,
        mesh=fine,
        in_specs=(P(LAG, ROW), P(LAG, ROW, None), P(LAG, ROW)),
        out_specs=P(LAG, ROW),
        check_vma=False,
    )
```

```python
import jax
import jax.numpy as jnp
from jax import lax
from jax.experimental import pallas as pl
from jax.experimental.pallas import tpu as pltpu
from jax.sharding import Mesh, PartitionSpec as P

B = 128
HALO = 16
LAGS = 16
LAG = ("x", "yl", "c")
ROW = ("yh", "zh", "zl")
TRADE = ("x", "yl", "zl")
COPIES = ("yh", "zh")


def swap_pairs(step):
    pairs = []
    for lag in range(16 - step):
        for row in range(32):
            x, yl, c = (lag + step) // 4, (lag + step) // 2 % 2, (lag + step) % 2
            yh, zh, zl = row // 8, row // 2 % 4, row % 2
            to_lag = (yh * 2 + zh % 2) * 2 + c
            to_row = x * 8 + (zh // 2 * 2 + yl) * 2 + zl
            pairs.append((lag * 32 + row, to_lag * 32 + to_row))
    return pairs


def split_kernel(p_ref, o_ref, in_ref, out_ref, in_sem, out_sem):
    parts = 4
    rows = B // parts
    loads = [pltpu.make_async_copy(p_ref.at[0, pl.ds(i * rows, rows)], in_ref.at[pl.ds(i * rows, rows)], in_sem.at[i]) for i in range(parts)]
    for load in loads:
        load.start()
    stores = []
    for i in range(parts):
        loads[i].wait()
        here = slice(i * rows, (i + 1) * rows)
        for x in range(4):
            for yl in range(2):
                for zl in range(2):
                    for h in range(2):
                        col = (x * 8 + h * 4 + yl * 2 + zl) * B
                        out_ref[(x * 2 + yl) * 2 + zl, here, h * B:(h + 1) * B] = in_ref[here, col:col + B]
        stores.append(pltpu.make_async_copy(out_ref.at[:, pl.ds(i * rows, rows)], o_ref.at[:, pl.ds(i * rows, rows)], out_sem.at[i]))
        stores[i].start()
    for store in stores:
        store.wait()


def split_panels(panels):
    anywhere = pl.BlockSpec(memory_space=pl.ANY)
    return pl.pallas_call(
        split_kernel,
        out_shape=jax.ShapeDtypeStruct((16, B, 2 * B), jnp.bfloat16),
        in_specs=[anywhere],
        out_specs=anywhere,
        scratch_shapes=[
            pltpu.VMEM((B, 32 * B), jnp.bfloat16),
            pltpu.VMEM((16, B, 2 * B), jnp.bfloat16),
            pltpu.SemaphoreType.DMA((4,)),
            pltpu.SemaphoreType.DMA((4,)),
        ],
        name="split",
    )(panels)


def field_kernel(c_ref, own_ref, other_ref, x_ref, h_ref, e_ref, out_ref, kept_ref, s_ref):
    core = c_ref[0]
    kept_ref[...] = e_ref[...]

    def place(m, h):
        return (m // 2) * 4 + h * 2 + m % 2

    def run(c):
        for m in range(8):
            for h in range(2):
                cols = slice(h * B, (h + 1) * B)
                before = m - 1 + c
                if before < 0:
                    s_ref[m, 0:HALO, cols] = jnp.zeros((HALO, B), jnp.float32)
                else:
                    s_ref[m, 0:HALO, cols] = h_ref[place(before, h)].astype(jnp.float32)
                s_ref[m, HALO:, cols] = x_ref[place(m, h)].astype(jnp.float32)
        acc = jnp.zeros((8 * B, 2 * B), jnp.float32)
        for k in range(LAGS):
            w_ref = own_ref if k % 2 == c else other_ref
            shifted = s_ref[:, HALO - k:HALO - k + B, :].astype(jnp.bfloat16).reshape(8 * B, 2 * B)
            acc += lax.dot_general(shifted, w_ref[k // 2], (((1,), (1,)), ((), ())), preferred_element_type=jnp.float32)
        for m in range(8):
            for zl in range(2):
                out_ref[m * 2 + zl] = acc[m * B:(m + 1) * B, zl * B:(zl + 1) * B]

    pl.when(core == 0)(lambda: run(0))
    pl.when(core == 1)(lambda: run(1))


def field_of(core, own, other, x, ends, excitation):
    vmem = pl.BlockSpec(memory_space=pltpu.VMEM)
    return pl.pallas_call(
        field_kernel,
        out_shape=(jax.ShapeDtypeStruct((16, B, B), jnp.float32), jax.ShapeDtypeStruct((B, B), jnp.float32)),
        in_specs=[pl.BlockSpec(memory_space=pltpu.SMEM)] + [vmem] * 5,
        out_specs=(vmem, vmem),
        scratch_shapes=[pltpu.VMEM((8, HALO + B, 2 * B), jnp.float32)],
        compiler_params=pltpu.CompilerParams(vmem_limit_bytes=48 * 1024 * 1024),
        name="field",
    )(core, own, other, x, ends, excitation)


def body(currents, panels, excitation):
    everyone = LAG + ROW
    own = lax.all_to_all(split_panels(panels), TRADE, 0, 0, tiled=True).reshape(8, 2 * B, 2 * B)
    block = lax.ppermute(currents, everyone, swap_pairs(0))
    x = lax.all_to_all(jnp.broadcast_to(block[None], (16,) + block.shape), COPIES, 0, 0, tiled=True)
    ends = lax.ppermute(x[:, B - HALO:], "c", [(0, 1), (1, 0)])
    other = lax.ppermute(own, "c", [(0, 1), (1, 0)])
    core = lax.axis_index("c").astype(jnp.int32).reshape(1)
    part, kept = field_of(core, own, other, x, ends, excitation)
    got = lax.all_to_all(part.astype(jnp.float16), TRADE, 0, 0, tiled=True)
    return kept - jnp.sum(got.astype(jnp.float32), 0)


def solution(mesh):
    fine = Mesh(mesh.devices.reshape(4, 2, 2, 4, 4, 2), LAG + ROW)
    return jax.shard_map(
        body,
        mesh=fine,
        in_specs=(P(LAG, ROW), P(LAG, ROW, None), P(LAG, ROW)),
        out_specs=P(LAG, ROW),
        check_vma=False,
    )
```

```python
import jax
import jax.numpy as jnp
from jax import lax
from jax.experimental import pallas as pl
from jax.experimental.pallas import tpu as pltpu
from jax.sharding import Mesh, PartitionSpec as P

B = 128
HALO = 16
LAGS = 16
LAG = ("x", "yl", "c")
ROW = ("yh", "zh", "zl")
TRADE = ("x", "yl", "zl")


def spot(x, qy, c, yh, zh, qz):
    lag = (x * 2 + (qy ^ yh // 2)) * 2 + c
    return lag * 32 + (yh * 4 + zh) * 2 + (qz ^ zh // 2)


def copy_groups():
    return [
        [spot(x, qy, c, yh, zh, qz) for yh in range(4) for zh in range(4)]
        for x in range(4) for qy in range(2) for c in range(2) for qz in range(2)
    ]


def swap_pairs():
    pairs = []
    for lag in range(16):
        for row in range(32):
            x, yl, c = lag // 4, lag // 2 % 2, lag % 2
            yh, zh, zl = row // 8, row // 2 % 4, row % 2
            to_zh = zh // 2 * 2 + yl
            pairs.append((lag * 32 + row, spot(yh, zh % 2, c, x, to_zh, zl ^ zh // 2)))
    return pairs


def split_kernel(flip_ref, p_ref, o_ref, in_ref, out_ref, at_ref, in_sem, out_sem, at_sem):
    parts = 4
    fetch = pltpu.make_async_copy(flip_ref, at_ref, at_sem)
    fetch.start()
    rows = B // parts
    loads = [pltpu.make_async_copy(p_ref.at[0, pl.ds(i * rows, rows)], in_ref.at[pl.ds(i * rows, rows)], in_sem.at[i]) for i in range(parts)]
    for load in loads:
        load.start()
    fetch.wait()
    flip = at_ref[0]
    stores = []
    for i in range(parts):
        loads[i].wait()
        here = slice(i * rows, (i + 1) * rows)
        for x in range(4):
            for qy in range(2):
                for qz in range(2):
                    to = x * 4 + ((qy * 2 + qz) ^ flip)
                    for h in range(2):
                        col = (x * 8 + h * 4 + qy * 2 + (qz ^ h)) * B
                        out_ref[to, here, h * B:(h + 1) * B] = in_ref[here, col:col + B]
        stores.append(pltpu.make_async_copy(out_ref.at[:, pl.ds(i * rows, rows)], o_ref.at[:, pl.ds(i * rows, rows)], out_sem.at[i]))
        stores[i].start()
    for store in stores:
        store.wait()


def split_panels(flip, panels):
    anywhere = pl.BlockSpec(memory_space=pl.ANY)
    return pl.pallas_call(
        split_kernel,
        out_shape=jax.ShapeDtypeStruct((16, B, 2 * B), jnp.bfloat16),
        in_specs=[anywhere, anywhere],
        out_specs=anywhere,
        scratch_shapes=[
            pltpu.VMEM((B, 32 * B), jnp.bfloat16),
            pltpu.VMEM((16, B, 2 * B), jnp.bfloat16),
            pltpu.SMEM((1,), jnp.int32),
            pltpu.SemaphoreType.DMA((4,)),
            pltpu.SemaphoreType.DMA((4,)),
            pltpu.SemaphoreType.DMA,
        ],
        name="split",
    )(flip, panels)


def field_kernel(c_ref, own_ref, other_ref, x_ref, h_ref, e_ref, out_ref, kept_ref, s_ref):
    core = c_ref[0]
    kept_ref[...] = e_ref[...]

    def place(m, h):
        return (m // 2) * 4 + h * 2 + m % 2

    def run(c):
        for m in range(8):
            for h in range(2):
                cols = slice(h * B, (h + 1) * B)
                before = m - 1 + c
                if before < 0:
                    s_ref[m, 0:HALO, cols] = jnp.zeros((HALO, B), jnp.float32)
                else:
                    s_ref[m, 0:HALO, cols] = h_ref[place(before, h)].astype(jnp.float32)
                s_ref[m, HALO:, cols] = x_ref[place(m, h)].astype(jnp.float32)
        acc = jnp.zeros((8 * B, 2 * B), jnp.float32)
        for k in range(LAGS):
            w_ref = own_ref if k % 2 == c else other_ref
            shifted = s_ref[:, HALO - k:HALO - k + B, :].astype(jnp.bfloat16).reshape(8 * B, 2 * B)
            acc += lax.dot_general(shifted, w_ref[k // 2], (((1,), (1,)), ((), ())), preferred_element_type=jnp.float32)
        for m in range(8):
            for zl in range(2):
                out_ref[m * 2 + zl] = acc[m * B:(m + 1) * B, zl * B:(zl + 1) * B]

    pl.when(core == 0)(lambda: run(0))
    pl.when(core == 1)(lambda: run(1))


def field_of(core, own, other, x, ends, excitation):
    vmem = pl.BlockSpec(memory_space=pltpu.VMEM)
    return pl.pallas_call(
        field_kernel,
        out_shape=(jax.ShapeDtypeStruct((16, B, B), jnp.float32), jax.ShapeDtypeStruct((B, B), jnp.float32)),
        in_specs=[pl.BlockSpec(memory_space=pltpu.SMEM)] + [vmem] * 5,
        out_specs=(vmem, vmem),
        scratch_shapes=[pltpu.VMEM((8, HALO + B, 2 * B), jnp.float32)],
        compiler_params=pltpu.CompilerParams(vmem_limit_bytes=48 * 1024 * 1024),
        name="field",
    )(core, own, other, x, ends, excitation)


def body(currents, panels, excitation):
    everyone = LAG + ROW
    core = lax.axis_index("c").astype(jnp.int32).reshape(1)
    flip = (lax.axis_index("yh") // 2 * 2 + lax.axis_index("zh") // 2).astype(jnp.int32).reshape(1)
    own = lax.all_to_all(split_panels(flip, panels), TRADE, 0, 0, tiled=True).reshape(8, 2 * B, 2 * B)
    block = lax.ppermute(currents, everyone, swap_pairs())
    copies = jnp.broadcast_to(block[None], (16,) + block.shape)
    x = lax.all_to_all(copies, everyone, 0, 0, tiled=True, axis_index_groups=copy_groups())
    ends = lax.ppermute(x[:, B - HALO:], "c", [(0, 1), (1, 0)])
    other = lax.ppermute(own, "c", [(0, 1), (1, 0)])
    part, kept = field_of(core, own, other, x, ends, excitation)
    got = lax.all_to_all(part.astype(jnp.float16), TRADE, 0, 0, tiled=True)
    return kept - jnp.sum(got.astype(jnp.float32), 0)


def solution(mesh):
    fine = Mesh(mesh.devices.reshape(4, 2, 2, 4, 4, 2), LAG + ROW)
    return jax.shard_map(
        body,
        mesh=fine,
        in_specs=(P(LAG, ROW), P(LAG, ROW, None), P(LAG, ROW)),
        out_specs=P(LAG, ROW),
        check_vma=False,
    )
```

```python
import jax
import jax.numpy as jnp
from jax import lax
from jax.experimental import pallas as pl
from jax.experimental.pallas import tpu as pltpu
from jax.sharding import Mesh, PartitionSpec as P

B = 128
HALO = 16
LAGS = 16
LAG = ("x", "yl", "c")
ROW = ("yh", "zh", "zl")
TRADE = ("x", "yl", "zl")
SETS = (
    (0, 29), (4, 25), (8, 21), (9, 20),
    (1, 30), (5, 26), (10, 23), (11, 22),
    (2, 31), (6, 27), (13, 16), (12, 17),
    (3, 24), (7, 28), (15, 18), (14, 19),
)
HOLDS = (
    (8, 5, 1, 7, 0, 4, 3, 12, 9, 13, 10, 15, 14, 2, 11, 6),
    (10, 7, 14, 1, 2, 6, 3, 5, 11, 4, 8, 13, 12, 0, 9, 15),
    (1, 12, 0, 8, 4, 7, 3, 5, 9, 13, 11, 6, 10, 14, 2, 15),
    (3, 12, 4, 5, 0, 8, 1, 7, 2, 15, 6, 13, 10, 14, 11, 9),
    (13, 4, 9, 7, 12, 5, 1, 0, 10, 2, 8, 6, 11, 3, 15, 14),
    (15, 6, 11, 5, 14, 7, 3, 2, 8, 0, 10, 4, 9, 1, 13, 12),
    (1, 13, 2, 6, 0, 4, 5, 9, 10, 8, 3, 14, 7, 12, 11, 15),
    (1, 4, 0, 13, 2, 6, 5, 9, 10, 14, 3, 12, 8, 11, 7, 15),
    (1, 5, 0, 13, 2, 6, 9, 4, 11, 15, 8, 12, 10, 7, 3, 14),
    (3, 7, 2, 15, 0, 4, 11, 6, 9, 13, 10, 14, 8, 5, 1, 12),
    (2, 6, 10, 7, 1, 5, 3, 14, 8, 12, 9, 15, 0, 13, 4, 11),
    (2, 6, 1, 5, 3, 14, 10, 7, 8, 12, 9, 4, 0, 15, 11, 13),
    (2, 6, 1, 5, 0, 13, 14, 4, 11, 3, 8, 12, 9, 15, 10, 7),
    (0, 4, 3, 7, 2, 15, 12, 6, 9, 1, 10, 14, 11, 13, 8, 5),
    (0, 4, 3, 7, 11, 6, 2, 15, 8, 12, 9, 13, 1, 5, 10, 14),
    (3, 6, 7, 11, 2, 4, 0, 15, 8, 14, 9, 13, 5, 10, 1, 12),
)


def holder(s, c, piece):
    x, qy, qz = s // 4, s // 2 % 2, s % 2
    yh, zh = HOLDS[s][piece] // 4, HOLDS[s][piece] % 4
    lag = (x * 2 + (qy ^ yh // 2)) * 2 + c
    return lag * 32 + (yh * 4 + zh) * 2 + (qz ^ zh // 2)


def copy_groups():
    return [[holder(s, c, piece) for piece in range(16)] for s in range(16) for c in range(2)]


def swap_pairs():
    return [
        ((m * 2 + c) * 32 + SETS[s][h], holder(s, c, h * 8 + m))
        for s in range(16) for c in range(2) for h in range(2) for m in range(8)
    ]


def split_kernel(flip_ref, p_ref, o_ref, in_ref, out_ref, at_ref, in_sem, out_sem, at_sem):
    parts = 4
    fetch = pltpu.make_async_copy(flip_ref, at_ref, at_sem)
    fetch.start()
    rows = B // parts
    loads = [pltpu.make_async_copy(p_ref.at[0, pl.ds(i * rows, rows)], in_ref.at[pl.ds(i * rows, rows)], in_sem.at[i]) for i in range(parts)]
    for load in loads:
        load.start()
    fetch.wait()
    flip = at_ref[0]
    stores = []
    for i in range(parts):
        loads[i].wait()
        here = slice(i * rows, (i + 1) * rows)
        for x in range(4):
            for qy in range(2):
                for qz in range(2):
                    to = x * 4 + ((qy * 2 + qz) ^ flip)
                    for h in range(2):
                        col = SETS[x * 4 + qy * 2 + qz][h] * B
                        out_ref[to, here, h * B:(h + 1) * B] = in_ref[here, col:col + B]
        stores.append(pltpu.make_async_copy(out_ref.at[:, pl.ds(i * rows, rows)], o_ref.at[:, pl.ds(i * rows, rows)], out_sem.at[i]))
        stores[i].start()
    for store in stores:
        store.wait()


def split_panels(flip, panels):
    anywhere = pl.BlockSpec(memory_space=pl.ANY)
    return pl.pallas_call(
        split_kernel,
        out_shape=jax.ShapeDtypeStruct((16, B, 2 * B), jnp.bfloat16),
        in_specs=[anywhere, anywhere],
        out_specs=anywhere,
        scratch_shapes=[
            pltpu.VMEM((B, 32 * B), jnp.bfloat16),
            pltpu.VMEM((16, B, 2 * B), jnp.bfloat16),
            pltpu.SMEM((1,), jnp.int32),
            pltpu.SemaphoreType.DMA((4,)),
            pltpu.SemaphoreType.DMA((4,)),
            pltpu.SemaphoreType.DMA,
        ],
        name="split",
    )(flip, panels)


def field_kernel(c_ref, own_ref, other_ref, x_ref, h_ref, e_ref, out_ref, kept_ref, s_ref):
    core = c_ref[0]
    kept_ref[...] = e_ref[...]

    def place(m, h):
        return h * 8 + m

    def run(c):
        for m in range(8):
            for h in range(2):
                cols = slice(h * B, (h + 1) * B)
                before = m - 1 + c
                if before < 0:
                    s_ref[m, 0:HALO, cols] = jnp.zeros((HALO, B), jnp.float32)
                else:
                    s_ref[m, 0:HALO, cols] = h_ref[place(before, h)].astype(jnp.float32)
                s_ref[m, HALO:, cols] = x_ref[place(m, h)].astype(jnp.float32)
        acc = jnp.zeros((8 * B, 2 * B), jnp.float32)
        for k in range(LAGS):
            w_ref = own_ref if k % 2 == c else other_ref
            shifted = s_ref[:, HALO - k:HALO - k + B, :].astype(jnp.bfloat16).reshape(8 * B, 2 * B)
            acc += lax.dot_general(shifted, w_ref[k // 2], (((1,), (1,)), ((), ())), preferred_element_type=jnp.float32)
        for m in range(8):
            for zl in range(2):
                out_ref[m * 2 + zl] = acc[m * B:(m + 1) * B, zl * B:(zl + 1) * B]

    pl.when(core == 0)(lambda: run(0))
    pl.when(core == 1)(lambda: run(1))


def field_of(core, own, other, x, ends, excitation):
    vmem = pl.BlockSpec(memory_space=pltpu.VMEM)
    return pl.pallas_call(
        field_kernel,
        out_shape=(jax.ShapeDtypeStruct((16, B, B), jnp.float32), jax.ShapeDtypeStruct((B, B), jnp.float32)),
        in_specs=[pl.BlockSpec(memory_space=pltpu.SMEM)] + [vmem] * 5,
        out_specs=(vmem, vmem),
        scratch_shapes=[pltpu.VMEM((8, HALO + B, 2 * B), jnp.float32)],
        compiler_params=pltpu.CompilerParams(vmem_limit_bytes=48 * 1024 * 1024),
        name="field",
    )(core, own, other, x, ends, excitation)


def body(currents, panels, excitation):
    everyone = LAG + ROW
    core = lax.axis_index("c").astype(jnp.int32).reshape(1)
    flip = (lax.axis_index("yh") // 2 * 2 + lax.axis_index("zh") // 2).astype(jnp.int32).reshape(1)
    own = lax.all_to_all(split_panels(flip, panels), TRADE, 0, 0, tiled=True).reshape(8, 2 * B, 2 * B)
    block = lax.ppermute(currents, everyone, swap_pairs())
    copies = jnp.broadcast_to(block[None], (16,) + block.shape)
    x = lax.all_to_all(copies, everyone, 0, 0, tiled=True, axis_index_groups=copy_groups())
    ends = lax.ppermute(x[:, B - HALO:], "c", [(0, 1), (1, 0)])
    other = lax.ppermute(own, "c", [(0, 1), (1, 0)])
    part, kept = field_of(core, own, other, x, ends, excitation)
    got = lax.all_to_all(part.astype(jnp.float16), TRADE, 0, 0, tiled=True)
    return kept - jnp.sum(got.astype(jnp.float32), 0)


def solution(mesh):
    fine = Mesh(mesh.devices.reshape(4, 2, 2, 4, 4, 2), LAG + ROW)
    return jax.shard_map(
        body,
        mesh=fine,
        in_specs=(P(LAG, ROW), P(LAG, ROW, None), P(LAG, ROW)),
        out_specs=P(LAG, ROW),
        check_vma=False,
    )
```

```python
import jax
import jax.numpy as jnp
from jax import lax
from jax.experimental import pallas as pl
from jax.experimental.pallas import tpu as pltpu
from jax.sharding import Mesh, PartitionSpec as P

B = 128
HALO = 16
LAGS = 16
LAG = ("x", "yl", "c")
ROW = ("yh", "zh", "zl")
TRADE = ("x", "yl", "zl")
SETS = (
    (0, 29), (4, 25), (8, 21), (9, 20),
    (1, 30), (5, 26), (10, 23), (11, 22),
    (2, 31), (6, 27), (13, 16), (12, 17),
    (3, 24), (7, 28), (15, 18), (14, 19),
)
HOLDS = (
    (8, 5, 1, 7, 0, 4, 3, 12, 9, 13, 10, 15, 14, 2, 11, 6),
    (10, 7, 14, 1, 2, 6, 3, 5, 11, 4, 8, 13, 12, 0, 9, 15),
    (1, 12, 0, 8, 4, 7, 3, 5, 9, 13, 11, 6, 10, 14, 2, 15),
    (3, 12, 4, 5, 0, 8, 1, 7, 2, 15, 6, 13, 10, 14, 11, 9),
    (13, 4, 9, 7, 12, 5, 1, 0, 10, 2, 8, 6, 11, 3, 15, 14),
    (15, 6, 11, 5, 14, 7, 3, 2, 8, 0, 10, 4, 9, 1, 13, 12),
    (1, 13, 2, 6, 0, 4, 5, 9, 10, 8, 3, 14, 7, 12, 11, 15),
    (1, 4, 0, 13, 2, 6, 5, 9, 10, 14, 3, 12, 8, 11, 7, 15),
    (1, 5, 0, 13, 2, 6, 9, 4, 11, 15, 8, 12, 10, 7, 3, 14),
    (3, 7, 2, 15, 0, 4, 11, 6, 9, 13, 10, 14, 8, 5, 1, 12),
    (2, 6, 10, 7, 1, 5, 3, 14, 8, 12, 9, 15, 0, 13, 4, 11),
    (2, 6, 1, 5, 3, 14, 10, 7, 8, 12, 9, 4, 0, 15, 11, 13),
    (2, 6, 1, 5, 0, 13, 14, 4, 11, 3, 8, 12, 9, 15, 10, 7),
    (0, 4, 3, 7, 2, 15, 12, 6, 9, 1, 10, 14, 11, 13, 8, 5),
    (0, 4, 3, 7, 11, 6, 2, 15, 8, 12, 9, 13, 1, 5, 10, 14),
    (3, 6, 7, 11, 2, 4, 0, 15, 8, 14, 9, 13, 5, 10, 1, 12),
)


ORDER = (11, 15, 10, 14, 7, 3, 6, 2, 9, 13, 5, 8, 1, 12, 4, 0)


def holder(s, c, piece):
    x, qy, qz = s // 4, s // 2 % 2, s % 2
    yh, zh = HOLDS[s][piece] // 4, HOLDS[s][piece] % 4
    lag = (x * 2 + (qy ^ yh // 2)) * 2 + c
    return lag * 32 + (yh * 4 + zh) * 2 + (qz ^ zh // 2)


def copy_groups():
    return [[holder(s, c, HOLDS[s].index(spot)) for spot in ORDER] for s in range(16) for c in range(2)]


def packed(places):
    word = sum(ORDER.index(place) << 4 * i for i, place in enumerate(places))
    return word - (1 << 32) if word >= 1 << 31 else word


def swap_pairs():
    return [
        ((m * 2 + c) * 32 + SETS[s][h], holder(s, c, h * 8 + m))
        for s in range(16) for c in range(2) for h in range(2) for m in range(8)
    ]


def split_kernel(p_ref, o_ref, in_ref, out_ref, in_sem, out_sem):
    parts = 4
    rows = B // parts
    loads = [pltpu.make_async_copy(p_ref.at[0, pl.ds(i * rows, rows)], in_ref.at[pl.ds(i * rows, rows)], in_sem.at[i]) for i in range(parts)]
    for load in loads:
        load.start()
    flip = lax.axis_index("yh") // 2 * 2 + lax.axis_index("zh") // 2
    stores = []
    for i in range(parts):
        loads[i].wait()
        here = slice(i * rows, (i + 1) * rows)
        for x in range(4):
            for qy in range(2):
                for qz in range(2):
                    to = x * 4 + ((qy * 2 + qz) ^ flip)
                    for h in range(2):
                        col = SETS[x * 4 + qy * 2 + qz][h] * B
                        out_ref[to, here, h * B:(h + 1) * B] = in_ref[here, col:col + B]
        stores.append(pltpu.make_async_copy(out_ref.at[:, pl.ds(i * rows, rows)], o_ref.at[:, pl.ds(i * rows, rows)], out_sem.at[i]))
        stores[i].start()
    for store in stores:
        store.wait()


def split_panels(panels):
    anywhere = pl.BlockSpec(memory_space=pl.ANY)
    return pl.pallas_call(
        split_kernel,
        out_shape=jax.ShapeDtypeStruct((16, B, 2 * B), jnp.bfloat16),
        in_specs=[anywhere],
        out_specs=anywhere,
        scratch_shapes=[
            pltpu.VMEM((B, 32 * B), jnp.bfloat16),
            pltpu.VMEM((16, B, 2 * B), jnp.bfloat16),
            pltpu.SemaphoreType.DMA((4,)),
            pltpu.SemaphoreType.DMA((4,)),
        ],
        name="split",
    )(panels)


def field_kernel(own_ref, other_ref, x_ref, h_ref, e_ref, out_ref, kept_ref, s_ref):
    core = lax.axis_index("c")
    kept_ref[...] = e_ref[...]
    qy = lax.axis_index("yl") ^ lax.axis_index("yh") // 2
    qz = lax.axis_index("zl") ^ lax.axis_index("zh") // 2
    mine = lax.axis_index("x") * 4 + qy * 2 + qz
    words = []
    for h in range(2):
        word = jnp.int32(0)
        for s in range(16):
            word = jnp.where(mine == s, jnp.int32(packed(HOLDS[s][h * 8:h * 8 + 8])), word)
        words.append(word)

    def place(m, h):
        return (words[h] >> 4 * m) & 15

    def run(c):
        for m in range(8):
            for h in range(2):
                cols = slice(h * B, (h + 1) * B)
                before = m - 1 + c
                if before < 0:
                    s_ref[m, 0:HALO, cols] = jnp.zeros((HALO, B), jnp.float32)
                else:
                    s_ref[m, 0:HALO, cols] = h_ref[place(before, h)].astype(jnp.float32)
                s_ref[m, HALO:, cols] = x_ref[place(m, h)].astype(jnp.float32)
        acc = jnp.zeros((8 * B, 2 * B), jnp.float32)
        for k in range(LAGS):
            w_ref = own_ref if k % 2 == c else other_ref
            shifted = s_ref[:, HALO - k:HALO - k + B, :].astype(jnp.bfloat16).reshape(8 * B, 2 * B)
            acc += lax.dot_general(shifted, w_ref[k // 2], (((1,), (1,)), ((), ())), preferred_element_type=jnp.float32)
        for m in range(8):
            for zl in range(2):
                out_ref[m * 2 + zl] = acc[m * B:(m + 1) * B, zl * B:(zl + 1) * B]

    pl.when(core == 0)(lambda: run(0))
    pl.when(core == 1)(lambda: run(1))


def field_of(own, other, x, ends, excitation):
    vmem = pl.BlockSpec(memory_space=pltpu.VMEM)
    return pl.pallas_call(
        field_kernel,
        out_shape=(jax.ShapeDtypeStruct((16, B, B), jnp.float32), jax.ShapeDtypeStruct((B, B), jnp.float32)),
        in_specs=[vmem] * 5,
        out_specs=(vmem, vmem),
        scratch_shapes=[pltpu.VMEM((8, HALO + B, 2 * B), jnp.float32)],
        compiler_params=pltpu.CompilerParams(vmem_limit_bytes=48 * 1024 * 1024),
        name="field",
    )(own, other, x, ends, excitation)


def body(currents, panels, excitation):
    everyone = LAG + ROW
    own = lax.all_to_all(split_panels(panels), TRADE, 0, 0, tiled=True).reshape(8, 2 * B, 2 * B)
    block = lax.ppermute(currents, everyone, swap_pairs())
    copies = jnp.broadcast_to(block[None], (16,) + block.shape)
    x = lax.all_to_all(copies, everyone, 0, 0, tiled=True, axis_index_groups=copy_groups())
    ends = lax.ppermute(x[:, B - HALO:], "c", [(0, 1), (1, 0)])
    other = lax.ppermute(own, "c", [(0, 1), (1, 0)])
    part, kept = field_of(own, other, x, ends, excitation)
    got = lax.all_to_all(part.astype(jnp.float16), TRADE, 0, 0, tiled=True)
    return kept - jnp.sum(got.astype(jnp.float32), 0)


def solution(mesh):
    fine = Mesh(mesh.devices.reshape(4, 2, 2, 4, 4, 2), LAG + ROW)
    return jax.shard_map(
        body,
        mesh=fine,
        in_specs=(P(LAG, ROW), P(LAG, ROW, None), P(LAG, ROW)),
        out_specs=P(LAG, ROW),
        check_vma=False,
    )
```

```python
import jax
import jax.numpy as jnp
from jax import lax
from jax.experimental import pallas as pl
from jax.experimental.pallas import tpu as pltpu
from jax.sharding import Mesh, PartitionSpec as P

B = 128
HALO = 16
LAGS = 16
LAG = ("x", "yl", "c")
ROW = ("yh", "zh", "zl")
TRADE = ("x", "yl", "zl")
SETS = (
    (0, 29), (4, 25), (8, 21), (9, 20),
    (1, 30), (5, 26), (10, 23), (11, 22),
    (2, 31), (6, 27), (13, 16), (12, 17),
    (3, 24), (7, 28), (15, 18), (14, 19),
)
HOLDS = (
    (8, 5, 1, 7, 0, 4, 3, 12, 9, 13, 10, 15, 14, 2, 11, 6),
    (10, 7, 14, 1, 2, 6, 3, 5, 11, 4, 8, 13, 12, 0, 9, 15),
    (1, 12, 0, 8, 4, 7, 3, 5, 9, 13, 11, 6, 10, 14, 2, 15),
    (3, 12, 4, 5, 0, 8, 1, 7, 2, 15, 6, 13, 10, 14, 11, 9),
    (13, 4, 9, 7, 12, 5, 1, 0, 10, 2, 8, 6, 11, 3, 15, 14),
    (15, 6, 11, 5, 14, 7, 3, 2, 8, 0, 10, 4, 9, 1, 13, 12),
    (1, 13, 2, 6, 0, 4, 5, 9, 10, 8, 3, 14, 7, 12, 11, 15),
    (1, 4, 0, 13, 2, 6, 5, 9, 10, 14, 3, 12, 8, 11, 7, 15),
    (1, 5, 0, 13, 2, 6, 9, 4, 11, 15, 8, 12, 10, 7, 3, 14),
    (3, 7, 2, 15, 0, 4, 11, 6, 9, 13, 10, 14, 8, 5, 1, 12),
    (2, 6, 10, 7, 1, 5, 3, 14, 8, 12, 9, 15, 0, 13, 4, 11),
    (2, 6, 1, 5, 3, 14, 10, 7, 8, 12, 9, 4, 0, 15, 11, 13),
    (2, 6, 1, 5, 0, 13, 14, 4, 11, 3, 8, 12, 9, 15, 10, 7),
    (0, 4, 3, 7, 2, 15, 12, 6, 9, 1, 10, 14, 11, 13, 8, 5),
    (0, 4, 3, 7, 11, 6, 2, 15, 8, 12, 9, 13, 1, 5, 10, 14),
    (3, 6, 7, 11, 2, 4, 0, 15, 8, 14, 9, 13, 5, 10, 1, 12),
)


ORDER = (10, 14, 6, 2, 11, 15, 7, 3, 9, 13, 5, 1, 8, 12, 4, 0)


def holder(s, c, piece):
    x, qy, qz = s // 4, s // 2 % 2, s % 2
    yh, zh = HOLDS[s][piece] // 4, HOLDS[s][piece] % 4
    lag = (x * 2 + (qy ^ yh // 2)) * 2 + c
    return lag * 32 + (yh * 4 + zh) * 2 + (qz ^ zh // 2)


def copy_groups():
    return [[holder(s, c, HOLDS[s].index(spot)) for spot in ORDER] for s in range(16) for c in range(2)]


def packed(places):
    word = sum(ORDER.index(place) << 4 * i for i, place in enumerate(places))
    return word - (1 << 32) if word >= 1 << 31 else word


def swap_pairs():
    return [
        ((m * 2 + c) * 32 + SETS[s][h], holder(s, c, h * 8 + m))
        for s in range(16) for c in range(2) for h in range(2) for m in range(8)
    ]


def trade_groups():
    return [
        [((x * 2 + yl) * 2 + c) * 32 + rows * 2 + zl for x in (3, 2, 1, 0) for yl in (1, 0) for zl in (1, 0)]
        for c in range(2) for rows in range(16)
    ]


def split_kernel(p_ref, o_ref, in_ref, out_ref, in_sem, out_sem):
    parts = 4
    rows = B // parts
    loads = [pltpu.make_async_copy(p_ref.at[0, pl.ds(i * rows, rows)], in_ref.at[pl.ds(i * rows, rows)], in_sem.at[i]) for i in range(parts)]
    for load in loads:
        load.start()
    flip = lax.axis_index("yh") // 2 * 2 + lax.axis_index("zh") // 2
    stores = []
    for i in range(parts):
        loads[i].wait()
        here = slice(i * rows, (i + 1) * rows)
        for x in range(4):
            for qy in range(2):
                for qz in range(2):
                    to = 15 - (x * 4 + ((qy * 2 + qz) ^ flip))
                    for h in range(2):
                        col = SETS[x * 4 + qy * 2 + qz][h] * B
                        out_ref[to, here, h * B:(h + 1) * B] = in_ref[here, col:col + B]
        stores.append(pltpu.make_async_copy(out_ref.at[:, pl.ds(i * rows, rows)], o_ref.at[:, pl.ds(i * rows, rows)], out_sem.at[i]))
        stores[i].start()
    for store in stores:
        store.wait()


def split_panels(panels):
    anywhere = pl.BlockSpec(memory_space=pl.ANY)
    return pl.pallas_call(
        split_kernel,
        out_shape=jax.ShapeDtypeStruct((16, B, 2 * B), jnp.bfloat16),
        in_specs=[anywhere],
        out_specs=anywhere,
        scratch_shapes=[
            pltpu.VMEM((B, 32 * B), jnp.bfloat16),
            pltpu.VMEM((16, B, 2 * B), jnp.bfloat16),
            pltpu.SemaphoreType.DMA((4,)),
            pltpu.SemaphoreType.DMA((4,)),
        ],
        name="split",
    )(panels)


def field_kernel(own_ref, other_ref, x_ref, h_ref, e_ref, out_ref, kept_ref, s_ref):
    core = lax.axis_index("c")
    kept_ref[...] = e_ref[...]
    qy = lax.axis_index("yl") ^ lax.axis_index("yh") // 2
    qz = lax.axis_index("zl") ^ lax.axis_index("zh") // 2
    mine = lax.axis_index("x") * 4 + qy * 2 + qz
    words = []
    for h in range(2):
        word = jnp.int32(0)
        for s in range(16):
            word = jnp.where(mine == s, jnp.int32(packed(HOLDS[s][h * 8:h * 8 + 8])), word)
        words.append(word)

    def place(m, h):
        return (words[h] >> 4 * m) & 15

    def run(c):
        for m in range(8):
            for h in range(2):
                cols = slice(h * B, (h + 1) * B)
                before = m - 1 + c
                if before < 0:
                    s_ref[m, 0:HALO, cols] = jnp.zeros((HALO, B), jnp.float32)
                else:
                    s_ref[m, 0:HALO, cols] = h_ref[place(before, h)].astype(jnp.float32)
                s_ref[m, HALO:, cols] = x_ref[place(m, h)].astype(jnp.float32)
        acc = jnp.zeros((8 * B, 2 * B), jnp.float32)
        for k in range(LAGS):
            w_ref = own_ref if k % 2 == c else other_ref
            shifted = s_ref[:, HALO - k:HALO - k + B, :].astype(jnp.bfloat16).reshape(8 * B, 2 * B)
            acc += lax.dot_general(shifted, w_ref[7 - k // 2], (((1,), (1,)), ((), ())), preferred_element_type=jnp.float32)
        for m in range(8):
            for zl in range(2):
                out_ref[15 - m * 2 - zl] = acc[m * B:(m + 1) * B, (1 - zl) * B:(2 - zl) * B]

    pl.when(core == 0)(lambda: run(0))
    pl.when(core == 1)(lambda: run(1))


def field_of(own, other, x, ends, excitation):
    vmem = pl.BlockSpec(memory_space=pltpu.VMEM)
    return pl.pallas_call(
        field_kernel,
        out_shape=(jax.ShapeDtypeStruct((16, B, B), jnp.float32), jax.ShapeDtypeStruct((B, B), jnp.float32)),
        in_specs=[vmem] * 5,
        out_specs=(vmem, vmem),
        scratch_shapes=[pltpu.VMEM((8, HALO + B, 2 * B), jnp.float32)],
        compiler_params=pltpu.CompilerParams(vmem_limit_bytes=48 * 1024 * 1024),
        name="field",
    )(own, other, x, ends, excitation)


def body(currents, panels, excitation):
    everyone = LAG + ROW
    own = lax.all_to_all(split_panels(panels), everyone, 0, 0, tiled=True, axis_index_groups=trade_groups()).reshape(8, 2 * B, 2 * B)
    block = lax.ppermute(currents, everyone, swap_pairs())
    copies = jnp.broadcast_to(block[None], (16,) + block.shape)
    x = lax.all_to_all(copies, everyone, 0, 0, tiled=True, axis_index_groups=copy_groups())
    ends = lax.ppermute(x[:, B - HALO:], "c", [(0, 1), (1, 0)])
    other = lax.ppermute(own, "c", [(0, 1), (1, 0)])
    part, kept = field_of(own, other, x, ends, excitation)
    got = lax.all_to_all(part.astype(jnp.float16), everyone, 0, 0, tiled=True, axis_index_groups=trade_groups())
    return kept - jnp.sum(got.astype(jnp.float32), 0)


def solution(mesh):
    fine = Mesh(mesh.devices.reshape(4, 2, 2, 4, 4, 2), LAG + ROW)
    return jax.shard_map(
        body,
        mesh=fine,
        in_specs=(P(LAG, ROW), P(LAG, ROW, None), P(LAG, ROW)),
        out_specs=P(LAG, ROW),
        check_vma=False,
    )
```

```python
import jax
import jax.numpy as jnp
from jax import lax
from jax.experimental import pallas as pl
from jax.experimental.pallas import tpu as pltpu
from jax.sharding import Mesh, PartitionSpec as P

B = 128
HALO = 16
LAGS = 16
LAG = ("x", "yl", "c")
ROW = ("yh", "zh", "zl")
TRADE = ("x", "yl", "zl")
SETS = (
    (0, 29), (4, 25), (8, 21), (9, 20),
    (1, 30), (5, 26), (10, 23), (11, 22),
    (2, 31), (6, 27), (13, 16), (12, 17),
    (3, 24), (7, 28), (15, 18), (14, 19),
)
HOLDS = (
    (8, 5, 1, 7, 0, 4, 3, 12, 9, 13, 10, 15, 14, 2, 11, 6),
    (10, 7, 14, 1, 2, 6, 3, 5, 11, 4, 8, 13, 12, 0, 9, 15),
    (1, 12, 0, 8, 4, 7, 3, 5, 9, 13, 11, 6, 10, 14, 2, 15),
    (3, 12, 4, 5, 0, 8, 1, 7, 2, 15, 6, 13, 10, 14, 11, 9),
    (13, 4, 9, 7, 12, 5, 1, 0, 10, 2, 8, 6, 11, 3, 15, 14),
    (15, 6, 11, 5, 14, 7, 3, 2, 8, 0, 10, 4, 9, 1, 13, 12),
    (1, 13, 2, 6, 0, 4, 5, 9, 10, 8, 3, 14, 7, 12, 11, 15),
    (1, 4, 0, 13, 2, 6, 5, 9, 10, 14, 3, 12, 8, 11, 7, 15),
    (1, 5, 0, 13, 2, 6, 9, 4, 11, 15, 8, 12, 10, 7, 3, 14),
    (3, 7, 2, 15, 0, 4, 11, 6, 9, 13, 10, 14, 8, 5, 1, 12),
    (2, 6, 10, 7, 1, 5, 3, 14, 8, 12, 9, 15, 0, 13, 4, 11),
    (2, 6, 1, 5, 3, 14, 10, 7, 8, 12, 9, 4, 0, 15, 11, 13),
    (2, 6, 1, 5, 0, 13, 14, 4, 11, 3, 8, 12, 9, 15, 10, 7),
    (0, 4, 3, 7, 2, 15, 12, 6, 9, 1, 10, 14, 11, 13, 8, 5),
    (0, 4, 3, 7, 11, 6, 2, 15, 8, 12, 9, 13, 1, 5, 10, 14),
    (3, 6, 7, 11, 2, 4, 0, 15, 8, 14, 9, 13, 5, 10, 1, 12),
)


ORDERS = (
    (10, 14, 6, 2, 11, 15, 7, 3, 9, 13, 5, 1, 8, 12, 4, 0),
    (14, 10, 2, 6, 15, 11, 3, 7, 13, 9, 1, 5, 12, 8, 0, 4),
)


def holder(s, c, piece):
    x, qy, qz = s // 4, s // 2 % 2, s % 2
    yh, zh = HOLDS[s][piece] // 4, HOLDS[s][piece] % 4
    lag = (x * 2 + (qy ^ yh // 2)) * 2 + c
    return lag * 32 + (yh * 4 + zh) * 2 + (qz ^ zh // 2)


def copy_groups():
    return [[holder(s, c, HOLDS[s].index(spot)) for spot in ORDERS[s // 2 % 2]] for s in range(16) for c in range(2)]


def packed(s, places):
    word = sum(ORDERS[s // 2 % 2].index(place) << 4 * i for i, place in enumerate(places))
    return word - (1 << 32) if word >= 1 << 31 else word


def swap_pairs():
    return [
        ((m * 2 + c) * 32 + SETS[s][h], holder(s, c, h * 8 + m))
        for s in range(16) for c in range(2) for h in range(2) for m in range(8)
    ]


def trade_groups():
    return [
        [((x * 2 + yl) * 2 + c) * 32 + rows * 2 + zl for x in (3, 2, 1, 0) for yl in (1, 0) for zl in (1, 0)]
        for c in range(2) for rows in range(16)
    ]


def split_kernel(p_ref, o_ref, in_ref, out_ref, in_sem, out_sem):
    parts = 4
    rows = B // parts
    loads = [pltpu.make_async_copy(p_ref.at[0, pl.ds(i * rows, rows)], in_ref.at[pl.ds(i * rows, rows)], in_sem.at[i]) for i in range(parts)]
    for load in loads:
        load.start()
    flip = lax.axis_index("yh") // 2 * 2 + lax.axis_index("zh") // 2
    stores = []
    for i in range(parts):
        loads[i].wait()
        here = slice(i * rows, (i + 1) * rows)
        for x in range(4):
            for qy in range(2):
                for qz in range(2):
                    to = 15 - (x * 4 + ((qy * 2 + qz) ^ flip))
                    for h in range(2):
                        col = SETS[x * 4 + qy * 2 + qz][h] * B
                        out_ref[to, here, h * B:(h + 1) * B] = in_ref[here, col:col + B]
        stores.append(pltpu.make_async_copy(out_ref.at[:, pl.ds(i * rows, rows)], o_ref.at[:, pl.ds(i * rows, rows)], out_sem.at[i]))
        stores[i].start()
    for store in stores:
        store.wait()


def split_panels(panels):
    anywhere = pl.BlockSpec(memory_space=pl.ANY)
    return pl.pallas_call(
        split_kernel,
        out_shape=jax.ShapeDtypeStruct((16, B, 2 * B), jnp.bfloat16),
        in_specs=[anywhere],
        out_specs=anywhere,
        scratch_shapes=[
            pltpu.VMEM((B, 32 * B), jnp.bfloat16),
            pltpu.VMEM((16, B, 2 * B), jnp.bfloat16),
            pltpu.SemaphoreType.DMA((4,)),
            pltpu.SemaphoreType.DMA((4,)),
        ],
        name="split",
    )(panels)


def field_kernel(own_ref, other_ref, x_ref, h_ref, e_ref, out_ref, kept_ref, s_ref):
    core = lax.axis_index("c")
    kept_ref[...] = e_ref[...]
    qy = lax.axis_index("yl") ^ lax.axis_index("yh") // 2
    qz = lax.axis_index("zl") ^ lax.axis_index("zh") // 2
    mine = lax.axis_index("x") * 4 + qy * 2 + qz
    words = []
    for h in range(2):
        word = jnp.int32(0)
        for s in range(16):
            word = jnp.where(mine == s, jnp.int32(packed(s, HOLDS[s][h * 8:h * 8 + 8])), word)
        words.append(word)

    def place(m, h):
        return (words[h] >> 4 * m) & 15

    def run(c):
        for m in range(8):
            for h in range(2):
                cols = slice(h * B, (h + 1) * B)
                before = m - 1 + c
                if before < 0:
                    s_ref[m, 0:HALO, cols] = jnp.zeros((HALO, B), jnp.float32)
                else:
                    s_ref[m, 0:HALO, cols] = h_ref[place(before, h)].astype(jnp.float32)
                s_ref[m, HALO:, cols] = x_ref[place(m, h)].astype(jnp.float32)
        acc = jnp.zeros((8 * B, 2 * B), jnp.float32)
        for k in range(LAGS):
            w_ref = own_ref if k % 2 == c else other_ref
            shifted = s_ref[:, HALO - k:HALO - k + B, :].astype(jnp.bfloat16).reshape(8 * B, 2 * B)
            acc += lax.dot_general(shifted, w_ref[7 - k // 2], (((1,), (1,)), ((), ())), preferred_element_type=jnp.float32)
        for m in range(8):
            for zl in range(2):
                out_ref[15 - m * 2 - zl] = acc[m * B:(m + 1) * B, (1 - zl) * B:(2 - zl) * B]

    pl.when(core == 0)(lambda: run(0))
    pl.when(core == 1)(lambda: run(1))


def field_of(own, other, x, ends, excitation):
    vmem = pl.BlockSpec(memory_space=pltpu.VMEM)
    return pl.pallas_call(
        field_kernel,
        out_shape=(jax.ShapeDtypeStruct((16, B, B), jnp.float32), jax.ShapeDtypeStruct((B, B), jnp.float32)),
        in_specs=[vmem] * 5,
        out_specs=(vmem, vmem),
        scratch_shapes=[pltpu.VMEM((8, HALO + B, 2 * B), jnp.float32)],
        compiler_params=pltpu.CompilerParams(vmem_limit_bytes=48 * 1024 * 1024),
        name="field",
    )(own, other, x, ends, excitation)


def body(currents, panels, excitation):
    everyone = LAG + ROW
    own = lax.all_to_all(split_panels(panels), everyone, 0, 0, tiled=True, axis_index_groups=trade_groups()).reshape(8, 2 * B, 2 * B)
    block = lax.ppermute(currents, everyone, swap_pairs())
    copies = jnp.broadcast_to(block[None], (16,) + block.shape)
    x = lax.all_to_all(copies, everyone, 0, 0, tiled=True, axis_index_groups=copy_groups())
    ends = lax.ppermute(x[:, B - HALO:], "c", [(0, 1), (1, 0)])
    other = lax.ppermute(own, "c", [(0, 1), (1, 0)])
    part, kept = field_of(own, other, x, ends, excitation)
    got = lax.all_to_all(part.astype(jnp.float16), everyone, 0, 0, tiled=True, axis_index_groups=trade_groups())
    return kept - jnp.sum(got.astype(jnp.float32), 0)


def solution(mesh):
    fine = Mesh(mesh.devices.reshape(4, 2, 2, 4, 4, 2), LAG + ROW)
    return jax.shard_map(
        body,
        mesh=fine,
        in_specs=(P(LAG, ROW), P(LAG, ROW, None), P(LAG, ROW)),
        out_specs=P(LAG, ROW),
        check_vma=False,
    )
```

```python
import jax
import jax.numpy as jnp
from jax import lax
from jax.experimental import pallas as pl
from jax.experimental.pallas import tpu as pltpu
from jax.sharding import Mesh, PartitionSpec as P

B = 128
HALO = 16
LAGS = 16
LAG = ("x", "yl", "c")
ROW = ("yh", "zh", "zl")
TRADE = ("x", "yl", "zl")
SETS = (
    (0, 29), (4, 25), (8, 21), (9, 20),
    (1, 30), (5, 26), (10, 23), (11, 22),
    (2, 31), (6, 27), (13, 16), (12, 17),
    (3, 24), (7, 28), (15, 18), (14, 19),
)
HOLDS = (
    (8, 5, 1, 7, 0, 4, 3, 12, 9, 13, 10, 15, 14, 2, 11, 6),
    (10, 7, 14, 1, 2, 6, 3, 5, 11, 4, 8, 13, 12, 0, 9, 15),
    (1, 12, 0, 8, 4, 7, 3, 5, 9, 13, 11, 6, 10, 14, 2, 15),
    (3, 12, 4, 5, 0, 8, 1, 7, 2, 15, 6, 13, 10, 14, 11, 9),
    (13, 4, 9, 7, 12, 5, 1, 0, 10, 2, 8, 6, 11, 3, 15, 14),
    (15, 6, 11, 5, 14, 7, 3, 2, 8, 0, 10, 4, 9, 1, 13, 12),
    (1, 13, 2, 6, 0, 4, 5, 9, 10, 8, 3, 14, 7, 12, 11, 15),
    (1, 4, 0, 13, 2, 6, 5, 9, 10, 14, 3, 12, 8, 11, 7, 15),
    (1, 5, 0, 13, 2, 6, 9, 4, 11, 15, 8, 12, 10, 7, 3, 14),
    (3, 7, 2, 15, 0, 4, 11, 6, 9, 13, 10, 14, 8, 5, 1, 12),
    (2, 6, 10, 7, 1, 5, 3, 14, 8, 12, 9, 15, 0, 13, 4, 11),
    (2, 6, 1, 5, 3, 14, 10, 7, 8, 12, 9, 4, 0, 15, 11, 13),
    (2, 6, 1, 5, 0, 13, 14, 4, 11, 3, 8, 12, 9, 15, 10, 7),
    (0, 4, 3, 7, 2, 15, 12, 6, 9, 1, 10, 14, 11, 13, 8, 5),
    (0, 4, 3, 7, 11, 6, 2, 15, 8, 12, 9, 13, 1, 5, 10, 14),
    (3, 6, 7, 11, 2, 4, 0, 15, 8, 14, 9, 13, 5, 10, 1, 12),
)


ORDER = (10, 14, 6, 2, 11, 15, 7, 3, 9, 13, 5, 1, 8, 12, 4, 0)


def holder(s, c, piece):
    x, qy, qz = s // 4, s // 2 % 2, s % 2
    yh, zh = HOLDS[s][piece] // 4, HOLDS[s][piece] % 4
    lag = (x * 2 + (qy ^ yh // 2)) * 2 + c
    return lag * 32 + (yh * 4 + zh) * 2 + (qz ^ zh // 2)


def copy_groups():
    return [[holder(s, c, HOLDS[s].index(spot)) for spot in ORDER] for s in range(16) for c in range(2)]


def packed(places):
    word = sum(ORDER.index(place) << 4 * i for i, place in enumerate(places))
    return word - (1 << 32) if word >= 1 << 31 else word


def swap_pairs():
    return [
        ((m * 2 + c) * 32 + SETS[s][h], holder(s, c, h * 8 + m))
        for s in range(16) for c in range(2) for h in range(2) for m in range(8)
    ]


def trade_groups():
    return [
        [((x * 2 + yl) * 2 + c) * 32 + rows * 2 + zl for x in (3, 2, 1, 0) for yl in (1, 0) for zl in (1, 0)]
        for c in range(2) for rows in range(16)
    ]


def split_kernel(p_ref, o_ref, in_ref, out_ref, in_sem, out_sem):
    parts = 8
    rows = B // parts
    loads = [pltpu.make_async_copy(p_ref.at[0, pl.ds(i * rows, rows)], in_ref.at[pl.ds(i * rows, rows)], in_sem.at[i]) for i in range(parts)]
    for load in loads:
        load.start()
    flip = lax.axis_index("yh") // 2 * 2 + lax.axis_index("zh") // 2
    stores = []
    for i in range(parts):
        loads[i].wait()
        here = slice(i * rows, (i + 1) * rows)
        for x in range(4):
            for qy in range(2):
                for qz in range(2):
                    to = 15 - (x * 4 + ((qy * 2 + qz) ^ flip))
                    for h in range(2):
                        col = SETS[x * 4 + qy * 2 + qz][h] * B
                        out_ref[to, here, h * B:(h + 1) * B] = in_ref[here, col:col + B]
        stores.append(pltpu.make_async_copy(out_ref.at[:, pl.ds(i * rows, rows)], o_ref.at[:, pl.ds(i * rows, rows)], out_sem.at[i]))
        stores[i].start()
    for store in stores:
        store.wait()


def split_panels(panels):
    anywhere = pl.BlockSpec(memory_space=pl.ANY)
    return pl.pallas_call(
        split_kernel,
        out_shape=jax.ShapeDtypeStruct((16, B, 2 * B), jnp.bfloat16),
        in_specs=[anywhere],
        out_specs=anywhere,
        scratch_shapes=[
            pltpu.VMEM((B, 32 * B), jnp.bfloat16),
            pltpu.VMEM((16, B, 2 * B), jnp.bfloat16),
            pltpu.SemaphoreType.DMA((8,)),
            pltpu.SemaphoreType.DMA((8,)),
        ],
        name="split",
    )(panels)


def field_kernel(own_ref, other_ref, x_ref, h_ref, e_ref, out_ref, kept_ref, s_ref):
    core = lax.axis_index("c")
    kept_ref[...] = e_ref[...]
    qy = lax.axis_index("yl") ^ lax.axis_index("yh") // 2
    qz = lax.axis_index("zl") ^ lax.axis_index("zh") // 2
    mine = lax.axis_index("x") * 4 + qy * 2 + qz
    words = []
    for h in range(2):
        word = jnp.int32(0)
        for s in range(16):
            word = jnp.where(mine == s, jnp.int32(packed(HOLDS[s][h * 8:h * 8 + 8])), word)
        words.append(word)

    def place(m, h):
        return (words[h] >> 4 * m) & 15

    def run(c):
        for m in range(8):
            for h in range(2):
                cols = slice(h * B, (h + 1) * B)
                before = m - 1 + c
                if before < 0:
                    s_ref[m, 0:HALO, cols] = jnp.zeros((HALO, B), jnp.float32)
                else:
                    s_ref[m, 0:HALO, cols] = h_ref[place(before, h)].astype(jnp.float32)
                s_ref[m, HALO:, cols] = x_ref[place(m, h)].astype(jnp.float32)
        acc = jnp.zeros((8 * B, 2 * B), jnp.float32)
        for k in range(LAGS):
            w_ref = own_ref if k % 2 == c else other_ref
            shifted = s_ref[:, HALO - k:HALO - k + B, :].astype(jnp.bfloat16).reshape(8 * B, 2 * B)
            acc += lax.dot_general(shifted, w_ref[7 - k // 2], (((1,), (1,)), ((), ())), preferred_element_type=jnp.float32)
        for m in range(8):
            for zl in range(2):
                out_ref[15 - m * 2 - zl] = acc[m * B:(m + 1) * B, (1 - zl) * B:(2 - zl) * B]

    pl.when(core == 0)(lambda: run(0))
    pl.when(core == 1)(lambda: run(1))


def field_of(own, other, x, ends, excitation):
    vmem = pl.BlockSpec(memory_space=pltpu.VMEM)
    return pl.pallas_call(
        field_kernel,
        out_shape=(jax.ShapeDtypeStruct((16, B, B), jnp.float32), jax.ShapeDtypeStruct((B, B), jnp.float32)),
        in_specs=[vmem] * 5,
        out_specs=(vmem, vmem),
        scratch_shapes=[pltpu.VMEM((8, HALO + B, 2 * B), jnp.float32)],
        compiler_params=pltpu.CompilerParams(vmem_limit_bytes=48 * 1024 * 1024),
        name="field",
    )(own, other, x, ends, excitation)


def body(currents, panels, excitation):
    everyone = LAG + ROW
    own = lax.all_to_all(split_panels(panels), everyone, 0, 0, tiled=True, axis_index_groups=trade_groups()).reshape(8, 2 * B, 2 * B)
    block = lax.ppermute(currents, everyone, swap_pairs())
    copies = jnp.broadcast_to(block[None], (16,) + block.shape)
    x = lax.all_to_all(copies, everyone, 0, 0, tiled=True, axis_index_groups=copy_groups())
    ends = lax.ppermute(x[:, B - HALO:], "c", [(0, 1), (1, 0)])
    other = lax.ppermute(own, "c", [(0, 1), (1, 0)])
    part, kept = field_of(own, other, x, ends, excitation)
    got = lax.all_to_all(part.astype(jnp.float16), everyone, 0, 0, tiled=True, axis_index_groups=trade_groups())
    return kept - jnp.sum(got.astype(jnp.float32), 0)


def solution(mesh):
    fine = Mesh(mesh.devices.reshape(4, 2, 2, 4, 4, 2), LAG + ROW)
    return jax.shard_map(
        body,
        mesh=fine,
        in_specs=(P(LAG, ROW), P(LAG, ROW, None), P(LAG, ROW)),
        out_specs=P(LAG, ROW),
        check_vma=False,
    )
```
